32 devices in a mesh: grp: 4 (over z), sub: 8 (over y, x, core).
Axes of the slice: x: 2, y: 2, z: 4, core: 2. Of those that a mesh axis runs over, the one named last changes fastest.
Arguments:
- top_basis: bfloat16 [4, 512, 256], P('grp', 'sub'), may hold values from -0.375 to 0.375
- top_coeffs: bfloat16 [4, 256, 128], P('grp'), may hold values from -6 to 6
- top_coupling: float32 [4, 512, 512], P('grp')
- block_coupling: float32 [4, 8, 128, 512], P('grp', 'sub'), may hold values from -0.09375 to 0.09375
- block_basis: bfloat16 [4, 8, 128, 128], P('grp', 'sub'), may hold values from -0.5 to 0.5
- block_coeffs: bfloat16 [4, 8, 128, 128], P('grp', 'sub'), may hold values from -6 to 6
- sub_basis: bfloat16 [4, 8, 1536, 256], P('grp', 'sub'), may hold values from -0.375 to 0.375
- sub_coeffs: bfloat16 [4, 8, 256, 128], P('grp', 'sub'), may hold values from -6 to 6
- basis_widths: int32 [4, 8], P('grp', 'sub'), may hold values from 32 to 256
- constraint_modes: bfloat16 [4, 8, 1536, 512], P('grp', 'sub'), may hold values from -0.25 to 0.25
- adjacency: int32 [4, 8, 4], P('grp', 'sub'), may hold values from 0 to 4, as said below
Outputs:
- top_values: float32 [4, 512, 128], P('grp')
- block_values: bfloat16 [4, 8, 128, 128], P('grp', 'sub')
- interior: bfloat16 [4, 8, 1536, 128], P('grp', 'sub')
The draws below stay inside these ranges and needn't reach their ends.
Inputs may be any that keep to these rules, and one draw needn't show every extreme that they name: `adjacency`: the 4 entries of one substructure are different.
All inputs are finite; a program needn't handle non-finite values.
Results may differ from the reference program's by a relative error of at most 0.0044.
Values may be sent and summed in bfloat16 or wider, within the bound.
A program may use at most 64 MiB of HBM per device.

```python
import math
import jax
import jax.numpy as jnp
from jax import lax

M = 128
KT = 256
KB = 128
KS = 256
NT = 512
NB = 128
ADJ = 4
NI = 1536
CHAIN = 4
N_GRP = 4
N_SUB = 8


def draw_top_coupling(key, part):
    key_speed = jax.random.fold_in(key, 11)
    key_noise = jax.random.fold_in(key, 12)
    speed = jax.random.uniform(key_speed, (N_GRP, NT), jnp.float32, 0.5, 4.0)
    diagonal = jnp.exp(math.log(0.2) / CHAIN * speed)
    identity = jnp.eye(NT, dtype=jnp.float32)[None, :, :]
    noise = jax.random.normal(key_noise, (N_GRP, NT, NT), jnp.float32) * (0.2 / math.sqrt(NT))
    return identity * diagonal[:, :, None] + noise


def draw_basis_widths(key, part):
    key_width = jax.random.fold_in(key, 21)
    key_high = jax.random.fold_in(key, 22)
    key_low = jax.random.fold_in(key, 23)
    widths = jax.random.randint(key_width, (N_GRP * N_SUB,), KS // 8, KS + 1)
    high_pick = jax.random.randint(key_high, (), 0, N_GRP * N_SUB)
    low_pick = (high_pick + 1 + jax.random.randint(key_low, (), 0, N_GRP * N_SUB - 1)) % (N_GRP * N_SUB)
    places = jnp.arange(N_GRP * N_SUB)
    widths = jnp.where(places == high_pick, KS, widths)
    widths = jnp.where(places == low_pick, KS // 8, widths)
    return widths.reshape(N_GRP, N_SUB).astype(jnp.int32)


def draw_adjacency(key, part):
    key_order = jax.random.fold_in(key, 31)
    scores = jax.random.randint(key_order, (N_GRP, N_SUB, 5), 0, 1 << 20) * 8 + jnp.arange(5)
    order = jnp.argsort(scores, axis=-1)
    return order[..., :ADJ].astype(jnp.int32)


def level_of(stream_key, shape, cuts, low, top_value):
    loudness, own = 1.0, jax.random.fold_in(stream_key, 6)
    for dim, blocks in cuts:
        steps = jnp.exp(jax.random.uniform(jax.random.fold_in(own, dim), (blocks,), jnp.float32, low / len(cuts), top_value / len(cuts)))
        loudness = loudness * jnp.repeat(steps, shape[dim] // blocks).reshape([-1 if axis == dim else 1 for axis in range(len(shape))])
    return loudness


def centred(stream_key, dims, scale, reach, cuts=(), kind=jnp.bfloat16):
    factor_of = level_of(stream_key, dims, cuts, -0.22, 0.18) if cuts else 1.0
    drawn = jax.random.normal(stream_key, dims, jnp.float32) * scale * factor_of
    return jnp.minimum(jnp.maximum(drawn, -reach), reach).astype(kind)


def setup_inputs(seed: int = 0) -> dict:
    keys = jax.random.split(jax.random.key(seed), 12)
    top_basis = centred(keys[0], (N_GRP, NT, KT), KT ** -0.5, 0.375, ((0, 4), (1, 8)))
    top_coeffs = centred(keys[1], (N_GRP, KT, M), 1.0, 6.0, ((0, 4),))
    top_coupling = draw_top_coupling(jax.random.fold_in(keys[11], 71), 0)
    block_coupling = centred(keys[3], (N_GRP, N_SUB, NB, NT), (8 * NT) ** -0.5, 0.09375, ((0, 4), (1, 8)), jnp.float32)
    block_basis = centred(keys[4], (N_GRP, N_SUB, NB, KB), KB ** -0.5, 0.5, ((0, 4), (1, 8)))
    block_coeffs = centred(keys[5], (N_GRP, N_SUB, KB, M), 1.0, 6.0, ((0, 4), (1, 8)))
    sub_basis = centred(keys[6], (N_GRP, N_SUB, NI, KS), KS ** -0.5, 0.375, ((0, 4), (1, 8)))
    sub_coeffs = centred(keys[7], (N_GRP, N_SUB, KS, M), 1.0, 6.0, ((0, 4), (1, 8)))
    basis_widths = draw_basis_widths(jax.random.fold_in(keys[11], 71), 0)
    constraint_modes = centred(keys[9], (N_GRP, N_SUB, NI, ADJ * NB), (ADJ * NB) ** -0.5, 0.25, ((0, 4), (1, 8)))
    adjacency = draw_adjacency(jax.random.fold_in(keys[11], 71), 0)
    return dict(top_basis=top_basis, top_coeffs=top_coeffs, top_coupling=top_coupling, block_coupling=block_coupling, block_basis=block_basis, block_coeffs=block_coeffs, sub_basis=sub_basis, sub_coeffs=sub_coeffs, basis_widths=basis_widths, constraint_modes=constraint_modes, adjacency=adjacency)


def chain_turn(previous, pieces):
    coupling_now, own_now = pieces
    current = own_now + jnp.dot(coupling_now, previous, precision=lax.Precision.HIGHEST)
    return current, current


def group_interior(pieces):
    basis, coeffs, widths_here, modes, slots, blocks = pieces
    live_mask = lax.broadcasted_iota(jnp.int32, (1, KS, 1), 1) < widths_here[:, None, None]
    live_coeffs = jnp.where(live_mask, coeffs, jnp.zeros_like(coeffs))
    fixed_part = jnp.einsum("sik,skm->sim", basis.astype(jnp.float32), live_coeffs.astype(jnp.float32))
    places = jnp.arange(N_SUB, dtype=jnp.int32)[:, None]
    neighbour = (places + slots - 2) % N_SUB
    chosen = blocks[neighbour]
    linked = chosen.reshape(N_SUB, ADJ * NB, M).astype(jnp.float32)
    bound_part = jnp.einsum("sir,srm->sim", modes.astype(jnp.float32), linked)
    return (fixed_part + bound_part).astype(jnp.bfloat16)


def reference(top_basis, top_coeffs, top_coupling, block_coupling, block_basis, block_coeffs, sub_basis, sub_coeffs, basis_widths, constraint_modes, adjacency):
    top_own = jnp.einsum("gnk,gkm->gnm", top_basis.astype(jnp.float32), top_coeffs.astype(jnp.float32))
    start_value = jnp.zeros((NT, M), jnp.float32)
    unused, top_values = lax.scan(chain_turn, start_value, (top_coupling, top_own))
    own_block = jnp.einsum("gsnk,gskm->gsnm", block_basis.astype(jnp.float32), block_coeffs.astype(jnp.float32))
    from_top = jnp.einsum("gsnt,gtm->gsnm", block_coupling, top_values, precision=lax.Precision.HIGHEST)
    block_values = (own_block + from_top).astype(jnp.bfloat16)
    interior = lax.map(group_interior, (sub_basis, sub_coeffs, basis_widths, constraint_modes, adjacency, block_values))
    return top_values, block_values, interior
```

```python
import functools
import jax
import jax.numpy as jnp
from jax import lax
from jax.experimental import pallas as pl
from jax.experimental.pallas import tpu as pltpu
from jax.sharding import PartitionSpec as P

BF16 = jnp.bfloat16
F32 = jnp.float32
NT_DIMS = (((1,), (1,)), ((), ()))


def dot_nt(a, b):
    return lax.dot_general(a, b, NT_DIMS, preferred_element_type=F32)


def kernel(
    groups,
    subs,
    owners,
    tb_hbm,
    tc_hbm,
    c_hbm,
    bc_hbm,
    bb_hbm,
    bk_hbm,
    sb_hbm,
    sc_hbm,
    width_ref,
    cm_hbm,
    adj_ref,
    top_out,
    block_out,
    interior_out,
    tb,
    tc,
    c_in,
    c_hi,
    c_lo,
    bc_in,
    bc_hi,
    bc_lo,
    bb,
    bk,
    own_block,
    sb,
    sc,
    cm,
    fixed,
    pieces,
    gathered_own,
    v_prev,
    v_all,
    top_stage,
    cand,
    linked,
    result,
    in_sem,
    out_sem,
    a2a_send,
    a2a_recv,
    hop_send,
    hop_recv,
    gat_send,
    gat_recv,
    nb_send,
    nb_recv,
):
    g = lax.axis_index("grp")
    s = lax.axis_index("sub")
    rows = tb_hbm.shape[1]
    lane_rows = tb.shape[0]
    per = lane_rows // rows
    chunks = result.shape[0]

    tb[...] = jnp.zeros_like(tb)
    place = pl.multiple_of(lax.rem(s, per) * rows, rows)
    loads = [
        pltpu.make_async_copy(tb_hbm.at[0], tb.at[pl.ds(place, rows)], in_sem.at[0]),
        pltpu.make_async_copy(tc_hbm.at[0], tc, in_sem.at[1]),
        pltpu.make_async_copy(c_hbm.at[0], c_in, in_sem.at[2]),
        pltpu.make_async_copy(bc_hbm.at[0, 0], bc_in, in_sem.at[3]),
        pltpu.make_async_copy(bb_hbm.at[0, 0], bb, in_sem.at[4]),
        pltpu.make_async_copy(bk_hbm.at[0, 0], bk, in_sem.at[5]),
        pltpu.make_async_copy(sb_hbm.at[0, 0], sb, in_sem.at[6]),
        pltpu.make_async_copy(sc_hbm.at[0, 0], sc, in_sem.at[7]),
        pltpu.make_async_copy(cm_hbm.at[0, 0], cm, in_sem.at[8]),
    ]
    for load in loads:
        load.start()

    def peer(d):
        return lax.rem(s + d, subs)

    barrier = pltpu.get_barrier_semaphore()
    for d in range(1, subs):
        pl.semaphore_signal(barrier, 1, device_id=(g, peer(d)), device_id_type=pl.DeviceIdType.MESH)

    @pl.when(g > 0)
    def _():
        pl.semaphore_signal(barrier, 1, device_id=(g - 1, s), device_id_type=pl.DeviceIdType.MESH)

    @pl.when(g < groups - 1)
    def _():
        pl.semaphore_signal(barrier, 1, device_id=(g + 1, s), device_id_type=pl.DeviceIdType.MESH)

    loads[0].wait()
    loads[1].wait()
    own_rows = jnp.dot(tb[...], tc[...], preferred_element_type=F32).T
    pieces[...] = own_rows.reshape(pieces.shape)

    beside = jnp.where(g > 0, 1, 0) + jnp.where(g < groups - 1, 1, 0)
    pl.semaphore_wait(barrier, subs - 1 + beside)

    def remote(src, dst, send, recv, grp, sub):
        return pltpu.make_async_remote_copy(
            src_ref=src,
            dst_ref=dst,
            send_sem=send,
            recv_sem=recv,
            device_id=(grp, sub),
            device_id_type=pl.DeviceIdType.MESH,
        )

    def owner_only(index, action):
        if owners == subs:
            action()
        else:
            pl.when(index < owners)(action)

    def piece_copy(t):
        return remote(pieces.at[t], gathered_own.at[s], a2a_send.at[t], a2a_recv.at[s], g, t)

    for d in range(1, subs):
        t = peer(d)
        owner_only(t, lambda t=t: piece_copy(t).start())

    def keep_own():
        gathered_own[s] = pieces[s]

    owner_only(s, keep_own)

    loads[2].wait()
    c_full = c_in[...]
    high = c_full.astype(BF16)
    c_hi[...] = high
    c_lo[...] = (c_full - high.astype(F32)).astype(BF16)

    def gather_copy(t):
        return remote(v_all.at[s], v_all.at[s], gat_send.at[t], gat_recv.at[s], g, t)

    def hop_copy():
        return remote(v_all.at[s], v_prev, hop_send, hop_recv, g + 1, s)

    def chain():
        for d in range(1, subs):
            src = peer(d)
            remote(pieces.at[0], gathered_own.at[src], a2a_send.at[0], a2a_recv.at[src], g, src).wait_recv()
        parts = []
        for j in range(subs // per):
            total = gathered_own[j * per]
            for k in range(1, per):
                total = total + gathered_own[j * per + k]
            parts.append(total)
        own = jnp.concatenate(parts, axis=1)

        @pl.when(g == 0)
        def _():
            v_all[s] = own.astype(BF16)

        @pl.when(g > 0)
        def _():
            remote(v_all.at[s], v_prev, hop_send, hop_recv, g, s).wait_recv()
            before = v_prev[...]
            v_all[s] = (own + dot_nt(before, c_hi[...]) + dot_nt(before, c_lo[...])).astype(BF16)

        @pl.when(g < groups - 1)
        def _():
            hop_copy().start()

        for d in range(1, subs):
            gather_copy(peer(d)).start()

    loads[3].wait()
    b_full = bc_in[...]
    b_high = b_full.astype(BF16)
    bc_hi[...] = b_high
    bc_lo[...] = (b_full - b_high.astype(F32)).astype(BF16)
    loads[4].wait()
    loads[5].wait()
    own_block[...] = jnp.dot(bb[...], bk[...], preferred_element_type=F32)

    owner_only(s, chain)

    loads[6].wait()
    loads[7].wait()
    coeffs = sc[...]
    live = lax.broadcasted_iota(jnp.int32, coeffs.shape, 0) < width_ref[0, 0]
    coeffs = jnp.where(live, coeffs, jnp.zeros_like(coeffs))
    fixed[...] = jnp.dot(sb[...], coeffs, preferred_element_type=F32)

    def gather_wait(src):
        remote(v_all.at[src], v_all.at[src], gat_send.at[0], gat_recv.at[src], g, src).wait_recv()

    for d in range(1, subs):
        src = peer(d)
        owner_only(src, lambda src=src: gather_wait(src))
    v = v_all[...].reshape(-1, v_all.shape[2])
    block = own_block[...] + dot_nt(bc_hi[...], v) + dot_nt(bc_lo[...], v)
    cand[2] = block.astype(BF16)
    nb_copies = []
    for i, o in enumerate((0, 1, 3, 4)):
        t = lax.rem(s - o + 2 + subs, subs)
        nb_copies.append(remote(cand.at[2], cand.at[o], nb_send.at[i], nb_recv.at[i], g, t))
    for copy in nb_copies:
        copy.start()
    stores = [pltpu.make_async_copy(cand.at[2], block_out.at[0, 0], out_sem.at[chunks])]
    stores[0].start()
    top_stage[...] = v.astype(F32).T
    stores.append(pltpu.make_async_copy(top_stage, top_out.at[0], out_sem.at[chunks + 1]))
    stores[1].start()
    loads[8].wait()
    for copy in nb_copies:
        copy.wait_recv()
    size = cand.shape[1]
    for a in range(linked.shape[0] // size):
        linked[a * size:(a + 1) * size, :] = cand[adj_ref[0, 0, a]]
    step = result.shape[1]
    for i in range(chunks):
        here = slice(i * step, (i + 1) * step)
        bound = jnp.dot(cm[here, :], linked[...], preferred_element_type=F32)
        result[i] = (fixed[here, :] + bound).astype(BF16)
        store = pltpu.make_async_copy(result.at[i], interior_out.at[0, 0, pl.ds(i * step, step)], out_sem.at[i])
        store.start()
        stores.append(store)

    for d in range(1, subs):
        t = peer(d)
        owner_only(t, lambda t=t: piece_copy(t).wait_send())

    def sent():
        @pl.when(g < groups - 1)
        def _():
            hop_copy().wait_send()

        for d in range(1, subs):
            gather_copy(peer(d)).wait_send()

    owner_only(s, sent)
    for copy in nb_copies:
        copy.wait_send()
    for store in stores:
        store.wait()


def body(*args):
    tb, tc, c, bc, bb, bk, sb, sc, widths, cm, adj = args
    groups, subs = lax.axis_size("grp"), lax.axis_size("sub")
    nt, modes = c.shape[1], tc.shape[2]
    rows = tb.shape[1]
    cols = max(16, modes // subs)
    owners = modes // cols
    lane_rows = max(128, rows)
    per = lane_rows // rows
    nb, ni = bc.shape[2], sb.shape[2]
    slots = adj.shape[2]
    chunks = 4
    hbm = pl.BlockSpec(memory_space=pl.ANY)
    smem = pl.BlockSpec(memory_space=pltpu.SMEM)
    dma = pltpu.SemaphoreType.DMA
    vmem = pltpu.VMEM
    scratch = [
        vmem((lane_rows, tb.shape[2]), BF16),
        vmem(tc.shape[1:], BF16),
        vmem((nt, nt), F32),
        vmem((nt, nt), BF16),
        vmem((nt, nt), BF16),
        vmem((nb, nt), F32),
        vmem((nb, nt), BF16),
        vmem((nb, nt), BF16),
        vmem(bb.shape[2:], BF16),
        vmem(bk.shape[2:], BF16),
        vmem((nb, modes), F32),
        vmem(sb.shape[2:], BF16),
        vmem(sc.shape[2:], BF16),
        vmem(cm.shape[2:], BF16),
        vmem((ni, modes), F32),
        vmem((owners, cols, lane_rows), F32),
        vmem((subs, cols, lane_rows), F32),
        vmem((cols, nt), BF16),
        vmem((owners, cols, nt), BF16),
        vmem((nt, modes), F32),
        vmem((5, nb, modes), BF16),
        vmem((slots * nb, modes), BF16),
        vmem((chunks, ni // chunks, modes), BF16),
        dma((9,)),
        dma((chunks + 2,)),
        dma((owners,)),
        dma((subs,)),
        dma,
        dma,
        dma((subs,)),
        dma((owners,)),
        dma((4,)),
        dma((4,)),
    ]
    return pl.pallas_call(
        functools.partial(kernel, groups, subs, owners),
        out_shape=(
            jax.ShapeDtypeStruct((1, nt, modes), F32),
            jax.ShapeDtypeStruct((1, 1, nb, modes), BF16),
            jax.ShapeDtypeStruct((1, 1, ni, modes), BF16),
        ),
        in_specs=[hbm, hbm, hbm, hbm, hbm, hbm, hbm, hbm, smem, hbm, smem],
        out_specs=(hbm, hbm, hbm),
        scratch_shapes=scratch,
        compiler_params=pltpu.CompilerParams(
            collective_id=0, has_side_effects=True, vmem_limit_bytes=60 * 1024 * 1024
        ),
        cost_estimate=pl.CostEstimate(flops=500_000_000, bytes_accessed=5_000_000, transcendentals=0),
    )(*args)


def solution(mesh):
    placed = (
        P("grp", "sub", None),
        P("grp", None, None),
        P("grp", None, None),
        P("grp", "sub", None, None),
        P("grp", "sub", None, None),
        P("grp", "sub", None, None),
        P("grp", "sub", None, None),
        P("grp", "sub", None, None),
        P("grp", "sub"),
        P("grp", "sub", None, None),
        P("grp", "sub", None),
    )
    return jax.shard_map(
        body,
        mesh=mesh,
        in_specs=placed,
        out_specs=(P("grp", None, None), P("grp", "sub", None, None), P("grp", "sub", None, None)),
        check_vma=False,
    )
```

```python
import functools
import jax
import jax.numpy as jnp
from jax import lax
from jax.experimental import pallas as pl
from jax.experimental.pallas import tpu as pltpu
from jax.sharding import PartitionSpec as P

BF16 = jnp.bfloat16
F32 = jnp.float32
NT_DIMS = (((1,), (1,)), ((), ()))


def dot_nt(a, b):
    return lax.dot_general(a, b, NT_DIMS, preferred_element_type=F32)


def kernel(
    groups,
    subs,
    owners,
    tb_hbm,
    tc_hbm,
    c_hbm,
    bc_hbm,
    bb_hbm,
    bk_hbm,
    sb_hbm,
    sc_hbm,
    width_ref,
    cm_hbm,
    adj_ref,
    top_out,
    block_out,
    interior_out,
    tb,
    tc,
    c_in,
    c_hi,
    c_lo,
    bc_in,
    bc_hi,
    bc_lo,
    bb,
    bk,
    own_block,
    sb,
    sc,
    cm,
    fixed,
    pieces,
    gathered_own,
    v_prev,
    v_all,
    top_stage,
    cand,
    linked,
    result,
    in_sem,
    out_sem,
    a2a_send,
    a2a_recv,
    hop_send,
    hop_recv,
    gat_send,
    gat_recv,
    nb_send,
    nb_recv,
):
    g = lax.axis_index("grp")
    s = lax.axis_index("sub")
    rows = tb_hbm.shape[1]
    lane_rows = tb.shape[0]
    per = lane_rows // rows
    chunks = result.shape[0]

    tb[...] = jnp.zeros_like(tb)
    place = pl.multiple_of(lax.rem(s, per) * rows, rows)
    loads = [
        pltpu.make_async_copy(tb_hbm.at[0], tb.at[pl.ds(place, rows)], in_sem.at[0]),
        pltpu.make_async_copy(tc_hbm.at[0], tc, in_sem.at[1]),
        pltpu.make_async_copy(c_hbm.at[0], c_in, in_sem.at[2]),
        pltpu.make_async_copy(bc_hbm.at[0, 0], bc_in, in_sem.at[3]),
        pltpu.make_async_copy(bb_hbm.at[0, 0], bb, in_sem.at[4]),
        pltpu.make_async_copy(bk_hbm.at[0, 0], bk, in_sem.at[5]),
        pltpu.make_async_copy(sb_hbm.at[0, 0], sb, in_sem.at[6]),
        pltpu.make_async_copy(sc_hbm.at[0, 0], sc, in_sem.at[7]),
        pltpu.make_async_copy(cm_hbm.at[0, 0], cm, in_sem.at[8]),
    ]
    for load in loads:
        load.start()

    def peer(d):
        return lax.rem(s + d, subs)

    barrier = pltpu.get_barrier_semaphore()
    for d in range(1, subs):
        pl.semaphore_signal(barrier, 1, device_id=(g, peer(d)), device_id_type=pl.DeviceIdType.MESH)

    @pl.when(g > 0)
    def _():
        pl.semaphore_signal(barrier, 1, device_id=(g - 1, s), device_id_type=pl.DeviceIdType.MESH)

    @pl.when(g < groups - 1)
    def _():
        pl.semaphore_signal(barrier, 1, device_id=(g + 1, s), device_id_type=pl.DeviceIdType.MESH)

    loads[0].wait()
    loads[1].wait()
    own_rows = jnp.dot(tb[...], tc[...], preferred_element_type=F32).T
    pieces[...] = own_rows.reshape(pieces.shape)

    beside = jnp.where(g > 0, 1, 0) + jnp.where(g < groups - 1, 1, 0)
    pl.semaphore_wait(barrier, subs - 1 + beside)

    def remote(src, dst, send, recv, grp, sub):
        return pltpu.make_async_remote_copy(
            src_ref=src,
            dst_ref=dst,
            send_sem=send,
            recv_sem=recv,
            device_id=(grp, sub),
            device_id_type=pl.DeviceIdType.MESH,
        )

    def owner_only(index, action):
        if owners == subs:
            action()
        else:
            pl.when(index < owners)(action)

    def piece_copy(t):
        return remote(pieces.at[t], gathered_own.at[s], a2a_send.at[t], a2a_recv.at[s], g, t)

    for d in range(1, subs):
        t = peer(d)
        owner_only(t, lambda t=t: piece_copy(t).start())

    def keep_own():
        gathered_own[s] = pieces[s]

    owner_only(s, keep_own)

    loads[2].wait()
    c_full = c_in[...]
    high = c_full.astype(BF16)
    c_hi[...] = high
    c_lo[...] = (c_full - high.astype(F32)).astype(BF16)

    def gather_copy(t):
        return remote(v_all.at[s], v_all.at[s], gat_send.at[t], gat_recv.at[s], g, t)

    def hop_copy():
        return remote(v_all.at[s], v_prev, hop_send, hop_recv, g + 1, s)

    def chain():
        for d in range(1, subs):
            src = peer(d)
            remote(pieces.at[0], gathered_own.at[src], a2a_send.at[0], a2a_recv.at[src], g, src).wait_recv()
        parts = []
        for j in range(subs // per):
            total = gathered_own[j * per]
            for k in range(1, per):
                total = total + gathered_own[j * per + k]
            parts.append(total)
        own = jnp.concatenate(parts, axis=1)

        @pl.when(g == 0)
        def _():
            v_all[s] = own.astype(BF16)

        @pl.when(g > 0)
        def _():
            remote(v_all.at[s], v_prev, hop_send, hop_recv, g, s).wait_recv()
            before = v_prev[...]
            v_all[s] = (own + dot_nt(before, c_hi[...]) + dot_nt(before, c_lo[...])).astype(BF16)

        @pl.when(g < groups - 1)
        def _():
            hop_copy().start()

        for d in range(1, subs):
            gather_copy(peer(d)).start()

    loads[3].wait()
    b_full = bc_in[...]
    b_high = b_full.astype(BF16)
    bc_hi[...] = b_high
    bc_lo[...] = (b_full - b_high.astype(F32)).astype(BF16)
    loads[4].wait()
    loads[5].wait()
    own_block[...] = jnp.dot(bb[...], bk[...], preferred_element_type=F32)

    owner_only(s, chain)

    loads[6].wait()
    loads[7].wait()
    coeffs = sc[...]
    live = lax.broadcasted_iota(jnp.int32, coeffs.shape, 0) < width_ref[0, 0]
    coeffs = jnp.where(live, coeffs, jnp.zeros_like(coeffs))
    fixed[...] = jnp.dot(sb[...], coeffs, preferred_element_type=F32)

    def gather_wait(src):
        remote(v_all.at[src], v_all.at[src], gat_send.at[0], gat_recv.at[src], g, src).wait_recv()

    for d in range(1, subs):
        src = peer(d)
        owner_only(src, lambda src=src: gather_wait(src))
    v = v_all[...].reshape(-1, v_all.shape[2])
    block = own_block[...] + dot_nt(bc_hi[...], v) + dot_nt(bc_lo[...], v)
    cand[2] = block.astype(BF16)
    nb_copies = []
    for i, o in enumerate((0, 1, 3, 4)):
        t = lax.rem(s - o + 2 + subs, subs)
        nb_copies.append(remote(cand.at[2], cand.at[o], nb_send.at[i], nb_recv.at[i], g, t))
    for copy in nb_copies:
        copy.start()
    stores = [pltpu.make_async_copy(cand.at[2], block_out.at[0, 0], out_sem.at[chunks])]
    stores[0].start()
    top_stage[...] = v.astype(F32).T
    stores.append(pltpu.make_async_copy(top_stage, top_out.at[0], out_sem.at[chunks + 1]))
    stores[1].start()
    loads[8].wait()
    for copy in nb_copies:
        copy.wait_recv()
    size = cand.shape[1]
    for a in range(linked.shape[0] // size):
        linked[a * size:(a + 1) * size, :] = cand[adj_ref[0, 0, a]]
    step = result.shape[1]
    for i in range(chunks):
        here = slice(i * step, (i + 1) * step)
        bound = jnp.dot(cm[here, :], linked[...], preferred_element_type=F32)
        result[i] = (fixed[here, :] + bound).astype(BF16)
        store = pltpu.make_async_copy(result.at[i], interior_out.at[0, 0, pl.ds(i * step, step)], out_sem.at[i])
        store.start()
        stores.append(store)

    for d in range(1, subs):
        t = peer(d)
        owner_only(t, lambda t=t: piece_copy(t).wait_send())

    def sent():
        @pl.when(g < groups - 1)
        def _():
            hop_copy().wait_send()

        for d in range(1, subs):
            gather_copy(peer(d)).wait_send()

    owner_only(s, sent)
    for copy in nb_copies:
        copy.wait_send()
    for store in stores:
        store.wait()


def hand_over_kernel(top, block, interior, top_out, block_out, interior_out, sem):
    copies = []
    half = interior.shape[2] // 2
    pairs = [(top, top_out), (block, block_out)]
    for i in range(2):
        part = (0, 0, pl.ds(i * half, half))
        pairs.append((interior.at[part], interior_out.at[part]))
    for i, (source, target) in enumerate(pairs):
        copies.append(pltpu.make_async_copy(source, target, sem.at[i]))
        copies[-1].start()
    for copy in copies:
        copy.wait()


def hand_over(results):
    hbm = pl.BlockSpec(memory_space=pl.ANY)
    return pl.pallas_call(
        hand_over_kernel,
        out_shape=tuple(jax.ShapeDtypeStruct(r.shape, r.dtype) for r in results),
        in_specs=[hbm] * 3,
        out_specs=(hbm,) * 3,
        scratch_shapes=[pltpu.SemaphoreType.DMA((4,))],
        compiler_params=pltpu.CompilerParams(vmem_limit_bytes=8 * 1024 * 1024),
    )(*results)


def body(*args):
    tb, tc, c, bc, bb, bk, sb, sc, widths, cm, adj = args
    groups, subs = lax.axis_size("grp"), lax.axis_size("sub")
    nt, modes = c.shape[1], tc.shape[2]
    rows = tb.shape[1]
    cols = max(16, modes // subs)
    owners = modes // cols
    lane_rows = max(128, rows)
    per = lane_rows // rows
    nb, ni = bc.shape[2], sb.shape[2]
    slots = adj.shape[2]
    chunks = 4
    hbm = pl.BlockSpec(memory_space=pl.ANY)
    smem = pl.BlockSpec(memory_space=pltpu.SMEM)
    dma = pltpu.SemaphoreType.DMA
    vmem = pltpu.VMEM
    scratch = [
        vmem((lane_rows, tb.shape[2]), BF16),
        vmem(tc.shape[1:], BF16),
        vmem((nt, nt), F32),
        vmem((nt, nt), BF16),
        vmem((nt, nt), BF16),
        vmem((nb, nt), F32),
        vmem((nb, nt), BF16),
        vmem((nb, nt), BF16),
        vmem(bb.shape[2:], BF16),
        vmem(bk.shape[2:], BF16),
        vmem((nb, modes), F32),
        vmem(sb.shape[2:], BF16),
        vmem(sc.shape[2:], BF16),
        vmem(cm.shape[2:], BF16),
        vmem((ni, modes), F32),
        vmem((owners, cols, lane_rows), F32),
        vmem((subs, cols, lane_rows), F32),
        vmem((cols, nt), BF16),
        vmem((owners, cols, nt), BF16),
        vmem((nt, modes), F32),
        vmem((5, nb, modes), BF16),
        vmem((slots * nb, modes), BF16),
        vmem((chunks, ni // chunks, modes), BF16),
        dma((9,)),
        dma((chunks + 2,)),
        dma((owners,)),
        dma((subs,)),
        dma,
        dma,
        dma((subs,)),
        dma((owners,)),
        dma((4,)),
        dma((4,)),
    ]
    results = pl.pallas_call(
        functools.partial(kernel, groups, subs, owners),
        out_shape=(
            jax.ShapeDtypeStruct((1, nt, modes), F32),
            jax.ShapeDtypeStruct((1, 1, nb, modes), BF16),
            jax.ShapeDtypeStruct((1, 1, ni, modes), BF16),
        ),
        in_specs=[hbm, hbm, hbm, hbm, hbm, hbm, hbm, hbm, smem, hbm, smem],
        out_specs=(hbm, hbm, hbm),
        scratch_shapes=scratch,
        compiler_params=pltpu.CompilerParams(
            collective_id=0, has_side_effects=True, vmem_limit_bytes=24 * 1024 * 1024
        ),
        cost_estimate=pl.CostEstimate(flops=500_000_000, bytes_accessed=5_000_000, transcendentals=0),
    )(*[pltpu.with_memory_space_constraint(a, pltpu.HBM) if a.ndim > 2 and a.dtype != jnp.int32 else a for a in args])
    return hand_over(results)


def solution(mesh):
    placed = (
        P("grp", "sub", None),
        P("grp", None, None),
        P("grp", None, None),
        P("grp", "sub", None, None),
        P("grp", "sub", None, None),
        P("grp", "sub", None, None),
        P("grp", "sub", None, None),
        P("grp", "sub", None, None),
        P("grp", "sub"),
        P("grp", "sub", None, None),
        P("grp", "sub", None),
    )
    return jax.shard_map(
        body,
        mesh=mesh,
        in_specs=placed,
        out_specs=(P("grp", None, None), P("grp", "sub", None, None), P("grp", "sub", None, None)),
        check_vma=False,
    )
```

```python
import functools
import jax
import jax.numpy as jnp
from jax import lax
from jax.experimental import pallas as pl
from jax.experimental.pallas import tpu as pltpu
from jax.sharding import PartitionSpec as P

BF16 = jnp.bfloat16
F32 = jnp.float32
NT_DIMS = (((1,), (1,)), ((), ()))


def dot_nt(a, b):
    return lax.dot_general(a, b, NT_DIMS, preferred_element_type=F32)


def kernel(
    groups,
    subs,
    owners,
    tb_hbm,
    tc_hbm,
    c_hbm,
    bc_hbm,
    bb_hbm,
    bk_hbm,
    sb_hbm,
    sc_hbm,
    width_ref,
    cm_hbm,
    adj_ref,
    top_out,
    block_out,
    interior_out,
    tb,
    tc,
    c_in,
    c_hi,
    c_lo,
    bc_in,
    bc_hi,
    bc_lo,
    bb,
    bk,
    own_block,
    sb,
    sc,
    cm,
    fixed,
    pieces,
    gathered_own,
    v_prev,
    v_all,
    top_stage,
    cand,
    linked,
    result,
    in_sem,
    out_sem,
    a2a_send,
    a2a_recv,
    hop_send,
    hop_recv,
    gat_send,
    gat_recv,
    nb_send,
    nb_recv,
    gathered_before,
    ahead_send,
    ahead_recv,
):
    g = lax.axis_index("grp")
    s = lax.axis_index("sub")
    rows = tb_hbm.shape[1]
    lane_rows = tb.shape[0]
    per = lane_rows // rows
    chunks = result.shape[0]

    tb[...] = jnp.zeros_like(tb)
    place = pl.multiple_of(lax.rem(s, per) * rows, rows)
    loads = [
        pltpu.make_async_copy(tb_hbm.at[0], tb.at[pl.ds(place, rows)], in_sem.at[0]),
        pltpu.make_async_copy(tc_hbm.at[0], tc, in_sem.at[1]),
        pltpu.make_async_copy(c_hbm.at[0], c_in, in_sem.at[2]),
        pltpu.make_async_copy(bc_hbm.at[0, 0], bc_in, in_sem.at[3]),
        pltpu.make_async_copy(bb_hbm.at[0, 0], bb, in_sem.at[4]),
        pltpu.make_async_copy(bk_hbm.at[0, 0], bk, in_sem.at[5]),
        pltpu.make_async_copy(sb_hbm.at[0, 0], sb, in_sem.at[6]),
        pltpu.make_async_copy(sc_hbm.at[0, 0], sc, in_sem.at[7]),
        pltpu.make_async_copy(cm_hbm.at[0, 0], cm, in_sem.at[8]),
    ]
    for load in loads:
        load.start()

    def peer(d):
        return lax.rem(s + d, subs)

    barrier = pltpu.get_barrier_semaphore()
    for d in range(1, subs):
        pl.semaphore_signal(barrier, 1, device_id=(g, peer(d)), device_id_type=pl.DeviceIdType.MESH)

    def greet(grp, sub):
        pl.semaphore_signal(barrier, 1, device_id=(grp, sub), device_id_type=pl.DeviceIdType.MESH)

    @pl.when(g < min(groups, 2))
    def _():
        if groups > 1:
            for d in range(subs):
                greet(1 - g, peer(d))

    @pl.when(g > 1)
    def _():
        greet(g - 1, s)

    @pl.when((g > 0) & (g < groups - 1))
    def _():
        greet(g + 1, s)

    loads[0].wait()
    loads[1].wait()
    own_rows = jnp.dot(tb[...], tc[...], preferred_element_type=F32).T
    pieces[...] = own_rows.reshape(pieces.shape)

    front = subs if groups > 1 else 0
    beside = jnp.where(g > 1, 1, front) + jnp.where((g > 0) & (g < groups - 1), 1, 0)
    pl.semaphore_wait(barrier, subs - 1 + beside)

    def remote(src, dst, send, recv, grp, sub):
        return pltpu.make_async_remote_copy(
            src_ref=src,
            dst_ref=dst,
            send_sem=send,
            recv_sem=recv,
            device_id=(grp, sub),
            device_id_type=pl.DeviceIdType.MESH,
        )

    def owner_only(index, action):
        if owners == subs:
            action()
        else:
            pl.when(index < owners)(action)

    def piece_copy(t):
        return remote(pieces.at[t], gathered_own.at[s], a2a_send.at[t], a2a_recv.at[s], g, t)

    def ahead_copy(t):
        return remote(pieces.at[t], gathered_before.at[s], ahead_send.at[t], ahead_recv.at[s], 1, t)

    if groups > 1:
        @pl.when(g == 0)
        def _():
            for d in range(subs):
                t = peer(d)
                owner_only(t, lambda t=t: ahead_copy(t).start())

    for d in range(1, subs):
        t = peer(d)
        owner_only(t, lambda t=t: piece_copy(t).start())

    def keep_own():
        gathered_own[s] = pieces[s]

    owner_only(s, keep_own)

    def gather_copy(t):
        return remote(v_all.at[s], v_all.at[s], gat_send.at[t], gat_recv.at[s], g, t)

    def hop_copy():
        return remote(v_all.at[s], v_prev, hop_send, hop_recv, g + 1, s)

    def collect(ref):
        parts = []
        for j in range(subs // per):
            total = ref[j * per]
            for k in range(1, per):
                total = total + ref[j * per + k]
            parts.append(total)
        return jnp.concatenate(parts, axis=1)

    def chain():
        for d in range(1, subs):
            src = peer(d)
            remote(pieces.at[0], gathered_own.at[src], a2a_send.at[0], a2a_recv.at[src], g, src).wait_recv()
        own = collect(gathered_own)

        @pl.when(g == 0)
        def _():
            v_all[s] = own.astype(BF16)

        @pl.when(g == 1)
        def _():
            for d in range(subs):
                src = peer(d)
                remote(pieces.at[0], gathered_before.at[src], ahead_send.at[0], ahead_recv.at[src], g, src).wait_recv()
            v_prev[...] = collect(gathered_before).astype(BF16)

        @pl.when(g > 1)
        def _():
            remote(v_all.at[s], v_prev, hop_send, hop_recv, g, s).wait_recv()

        @pl.when(g > 0)
        def _():
            before = v_prev[...]
            v_all[s] = (own + jnp.dot(before, c_hi[...], preferred_element_type=F32) + jnp.dot(before, c_lo[...], preferred_element_type=F32)).astype(BF16)

        @pl.when((g > 0) & (g < groups - 1))
        def _():
            hop_copy().start()

        for d in range(1, subs):
            gather_copy(peer(d)).start()

    def local_work():
        loads[3].wait()
        b_full = bc_in[...]
        b_high = b_full.astype(BF16)
        bc_hi[...] = b_high
        bc_lo[...] = (b_full - b_high.astype(F32)).astype(BF16)
        loads[4].wait()
        loads[5].wait()
        own_block[...] = jnp.dot(bb[...], bk[...], preferred_element_type=F32)
        loads[6].wait()
        loads[7].wait()
        coeffs = sc[...]
        live = lax.broadcasted_iota(jnp.int32, coeffs.shape, 0) < width_ref[0, 0]
        coeffs = jnp.where(live, coeffs, jnp.zeros_like(coeffs))
        fixed[...] = jnp.dot(sb[...], coeffs, preferred_element_type=F32)

    @pl.when(g > 0)
    def _():
        loads[2].wait()
        c_full = c_in[...].T
        high = c_full.astype(BF16)
        c_hi[...] = high
        c_lo[...] = (c_full - high.astype(F32)).astype(BF16)
        local_work()

    owner_only(s, chain)

    @pl.when(g == 0)
    def _():
        loads[2].wait()
        local_work()

    def gather_wait(src):
        remote(v_all.at[src], v_all.at[src], gat_send.at[0], gat_recv.at[src], g, src).wait_recv()

    for d in range(1, subs):
        src = peer(d)
        owner_only(src, lambda src=src: gather_wait(src))
    v = v_all[...].reshape(-1, v_all.shape[2])
    block = own_block[...] + dot_nt(bc_hi[...], v) + dot_nt(bc_lo[...], v)
    cand[2] = block.astype(BF16)
    nb_copies = []
    for i, o in enumerate((0, 1, 3, 4)):
        t = lax.rem(s - o + 2 + subs, subs)
        nb_copies.append(remote(cand.at[2], cand.at[o], nb_send.at[i], nb_recv.at[i], g, t))
    for copy in nb_copies:
        copy.start()
    block_out[0, 0] = cand[2]
    top_out[0] = v.astype(F32).T
    loads[8].wait()
    for copy in nb_copies:
        copy.wait_recv()
    size = cand.shape[1]
    for a in range(linked.shape[0] // size):
        linked[a * size:(a + 1) * size, :] = cand[adj_ref[0, 0, a]]
    step = result.shape[1]
    for i in range(chunks):
        here = slice(i * step, (i + 1) * step)
        bound = jnp.dot(cm[here, :], linked[...], preferred_element_type=F32)
        interior_out[0, 0, here, :] = (fixed[here, :] + bound).astype(BF16)

    for d in range(1, subs):
        t = peer(d)
        owner_only(t, lambda t=t: piece_copy(t).wait_send())

    if groups > 1:
        @pl.when(g == 0)
        def _():
            for d in range(subs):
                t = peer(d)
                owner_only(t, lambda t=t: ahead_copy(t).wait_send())

    def sent():
        @pl.when((g > 0) & (g < groups - 1))
        def _():
            hop_copy().wait_send()

        for d in range(1, subs):
            gather_copy(peer(d)).wait_send()

    owner_only(s, sent)
    for copy in nb_copies:
        copy.wait_send()


def hand_over_kernel(top, block, interior, top_out, block_out, interior_out, sem):
    copies = []
    half = interior.shape[2] // 2
    pairs = [(top, top_out), (block, block_out)]
    for i in range(2):
        part = (0, 0, pl.ds(i * half, half))
        pairs.append((interior.at[part], interior_out.at[part]))
    for i, (source, target) in enumerate(pairs):
        copies.append(pltpu.make_async_copy(source, target, sem.at[i]))
        copies[-1].start()
    for copy in copies:
        copy.wait()


def hand_over(results):
    hbm = pl.BlockSpec(memory_space=pl.ANY)
    return pl.pallas_call(
        hand_over_kernel,
        out_shape=tuple(jax.ShapeDtypeStruct(r.shape, r.dtype) for r in results),
        in_specs=[hbm] * 3,
        out_specs=(hbm,) * 3,
        scratch_shapes=[pltpu.SemaphoreType.DMA((4,))],
        compiler_params=pltpu.CompilerParams(vmem_limit_bytes=8 * 1024 * 1024),
    )(*results)


def body(*args):
    tb, tc, c, bc, bb, bk, sb, sc, widths, cm, adj = args
    groups, subs = lax.axis_size("grp"), lax.axis_size("sub")
    nt, modes = c.shape[1], tc.shape[2]
    rows = tb.shape[1]
    cols = max(16, modes // subs)
    owners = modes // cols
    lane_rows = max(128, rows)
    per = lane_rows // rows
    nb, ni = bc.shape[2], sb.shape[2]
    slots = adj.shape[2]
    chunks = 4
    hbm = pl.BlockSpec(memory_space=pl.ANY)
    smem = pl.BlockSpec(memory_space=pltpu.SMEM)
    dma = pltpu.SemaphoreType.DMA
    vmem = pltpu.VMEM
    scratch = [
        vmem((lane_rows, tb.shape[2]), BF16),
        vmem(tc.shape[1:], BF16),
        vmem((nt, nt), F32),
        vmem((nt, nt), BF16),
        vmem((nt, nt), BF16),
        vmem((nb, nt), F32),
        vmem((nb, nt), BF16),
        vmem((nb, nt), BF16),
        vmem(bb.shape[2:], BF16),
        vmem(bk.shape[2:], BF16),
        vmem((nb, modes), F32),
        vmem(sb.shape[2:], BF16),
        vmem(sc.shape[2:], BF16),
        vmem(cm.shape[2:], BF16),
        vmem((ni, modes), F32),
        vmem((owners, cols, lane_rows), F32),
        vmem((subs, cols, lane_rows), F32),
        vmem((cols, nt), BF16),
        vmem((owners, cols, nt), BF16),
        vmem((nt, modes), F32),
        vmem((5, nb, modes), BF16),
        vmem((slots * nb, modes), BF16),
        vmem((chunks, ni // chunks, modes), BF16),
        dma((9,)),
        dma((chunks + 2,)),
        dma((owners,)),
        dma((subs,)),
        dma,
        dma,
        dma((subs,)),
        dma((owners,)),
        dma((4,)),
        dma((4,)),
        vmem((subs, cols, lane_rows), F32),
        dma((owners,)),
        dma((subs,)),
    ]
    results = pl.pallas_call(
        functools.partial(kernel, groups, subs, owners),
        out_shape=(
            jax.ShapeDtypeStruct((1, nt, modes), F32),
            jax.ShapeDtypeStruct((1, 1, nb, modes), BF16),
            jax.ShapeDtypeStruct((1, 1, ni, modes), BF16),
        ),
        in_specs=[hbm, hbm, hbm, hbm, hbm, hbm, hbm, hbm, smem, hbm, smem],
        out_specs=(pl.BlockSpec(memory_space=pltpu.VMEM),) * 3,
        scratch_shapes=scratch,
        compiler_params=pltpu.CompilerParams(
            collective_id=0, has_side_effects=True, vmem_limit_bytes=24 * 1024 * 1024
        ),
        cost_estimate=pl.CostEstimate(flops=500_000_000, bytes_accessed=5_000_000, transcendentals=0),
    )(*[pltpu.with_memory_space_constraint(a, pltpu.HBM) if a.ndim > 2 and a.dtype != jnp.int32 else a for a in args])
    return hand_over(results)


def solution(mesh):
    placed = (
        P("grp", "sub", None),
        P("grp", None, None),
        P("grp", None, None),
        P("grp", "sub", None, None),
        P("grp", "sub", None, None),
        P("grp", "sub", None, None),
        P("grp", "sub", None, None),
        P("grp", "sub", None, None),
        P("grp", "sub"),
        P("grp", "sub", None, None),
        P("grp", "sub", None),
    )
    return jax.shard_map(
        body,
        mesh=mesh,
        in_specs=placed,
        out_specs=(P("grp", None, None), P("grp", "sub", None, None), P("grp", "sub", None, None)),
        check_vma=False,
    )
```

```python
import functools
import jax
import jax.numpy as jnp
from jax import lax
from jax.experimental import pallas as pl
from jax.experimental.pallas import tpu as pltpu
from jax.sharding import PartitionSpec as P

BF16 = jnp.bfloat16
F32 = jnp.float32
NT_DIMS = (((1,), (1,)), ((), ()))


def dot_nt(a, b):
    return lax.dot_general(a, b, NT_DIMS, preferred_element_type=F32)


def kernel(
    groups,
    subs,
    owners,
    tb_hbm,
    tc_hbm,
    c_hbm,
    bc_hbm,
    bb_hbm,
    bk_hbm,
    sb_hbm,
    sc_hbm,
    width_ref,
    cm_hbm,
    adj_hbm,
    top_out,
    block_out,
    interior_out,
    tb,
    tc,
    c_in,
    c_hi,
    c_lo,
    bc_in,
    bc_hi,
    bc_lo,
    bb,
    bk,
    own_block,
    sb,
    sc,
    cm,
    fixed,
    pieces,
    gathered_own,
    v_prev,
    v_all,
    top_stage,
    cand,
    linked,
    result,
    in_sem,
    out_sem,
    a2a_send,
    a2a_recv,
    hop_send,
    hop_recv,
    gat_send,
    gat_recv,
    nb_send,
    nb_recv,
    gathered_before,
    ahead_send,
    ahead_recv,
    adj_ref,
):
    g = lax.axis_index("grp")
    s = lax.axis_index("sub")
    rows = tb_hbm.shape[1]
    lane_rows = tb.shape[0]
    per = lane_rows // rows
    chunks = result.shape[0]

    tb[...] = jnp.zeros_like(tb)
    place = pl.multiple_of(lax.rem(s, per) * rows, rows)
    loads = [
        pltpu.make_async_copy(tb_hbm.at[0], tb.at[pl.ds(place, rows)], in_sem.at[0]),
        pltpu.make_async_copy(tc_hbm.at[0], tc, in_sem.at[1]),
        pltpu.make_async_copy(c_hbm.at[0], c_in, in_sem.at[2]),
        pltpu.make_async_copy(bc_hbm.at[0, 0], bc_in, in_sem.at[3]),
        pltpu.make_async_copy(bb_hbm.at[0, 0], bb, in_sem.at[4]),
        pltpu.make_async_copy(bk_hbm.at[0, 0], bk, in_sem.at[5]),
        pltpu.make_async_copy(sb_hbm.at[0, 0], sb, in_sem.at[6]),
        pltpu.make_async_copy(sc_hbm.at[0, 0], sc, in_sem.at[7]),
        pltpu.make_async_copy(cm_hbm.at[0, 0], cm, in_sem.at[8]),
        pltpu.make_async_copy(adj_hbm, adj_ref, in_sem.at[9]),
    ]
    for load in loads:
        load.start()

    def peer(d):
        return lax.rem(s + d, subs)

    barrier = pltpu.get_barrier_semaphore()
    for d in range(1, subs):
        pl.semaphore_signal(barrier, 1, device_id=(g, peer(d)), device_id_type=pl.DeviceIdType.MESH)

    def greet(grp, sub):
        pl.semaphore_signal(barrier, 1, device_id=(grp, sub), device_id_type=pl.DeviceIdType.MESH)

    @pl.when(g < min(groups, 2))
    def _():
        if groups > 1:
            for d in range(subs):
                greet(1 - g, peer(d))

    @pl.when(g > 1)
    def _():
        greet(g - 1, s)

    @pl.when((g > 0) & (g < groups - 1))
    def _():
        greet(g + 1, s)

    loads[0].wait()
    loads[1].wait()
    own_rows = jnp.dot(tb[...], tc[...], preferred_element_type=F32).T
    pieces[...] = own_rows.reshape(pieces.shape)

    front = subs if groups > 1 else 0
    beside = jnp.where(g > 1, 1, front) + jnp.where((g > 0) & (g < groups - 1), 1, 0)
    pl.semaphore_wait(barrier, subs - 1 + beside)

    def remote(src, dst, send, recv, grp, sub):
        return pltpu.make_async_remote_copy(
            src_ref=src,
            dst_ref=dst,
            send_sem=send,
            recv_sem=recv,
            device_id=(grp, sub),
            device_id_type=pl.DeviceIdType.MESH,
        )

    def owner_only(index, action):
        if owners == subs:
            action()
        else:
            pl.when(index < owners)(action)

    def piece_copy(t):
        return remote(pieces.at[t], gathered_own.at[s], a2a_send.at[t], a2a_recv.at[s], g, t)

    def ahead_copy(t):
        return remote(pieces.at[t], gathered_before.at[s], ahead_send.at[t], ahead_recv.at[s], 1, t)

    if groups > 1:
        @pl.when(g == 0)
        def _():
            for d in range(subs):
                t = peer(d)
                owner_only(t, lambda t=t: ahead_copy(t).start())

    for d in range(1, subs):
        t = peer(d)
        owner_only(t, lambda t=t: piece_copy(t).start())

    def keep_own():
        gathered_own[s] = pieces[s]

    owner_only(s, keep_own)

    def gather_copy(t):
        return remote(v_all.at[s], v_all.at[s], gat_send.at[t], gat_recv.at[s], g, t)

    def hop_copy():
        return remote(v_all.at[s], v_prev, hop_send, hop_recv, g + 1, s)

    def collect(ref):
        parts = []
        for j in range(subs // per):
            total = ref[j * per]
            for k in range(1, per):
                total = total + ref[j * per + k]
            parts.append(total)
        return jnp.concatenate(parts, axis=1)

    def chain():
        for d in range(1, subs):
            src = peer(d)
            remote(pieces.at[0], gathered_own.at[src], a2a_send.at[0], a2a_recv.at[src], g, src).wait_recv()
        own = collect(gathered_own)

        @pl.when(g == 0)
        def _():
            v_all[s] = own.astype(BF16)

        @pl.when(g == 1)
        def _():
            for d in range(subs):
                src = peer(d)
                remote(pieces.at[0], gathered_before.at[src], ahead_send.at[0], ahead_recv.at[src], g, src).wait_recv()
            v_prev[...] = collect(gathered_before).astype(BF16)

        @pl.when(g > 1)
        def _():
            remote(v_all.at[s], v_prev, hop_send, hop_recv, g, s).wait_recv()

        @pl.when(g > 0)
        def _():
            before = v_prev[...]
            v_all[s] = (own + jnp.dot(before, c_hi[...], preferred_element_type=F32) + jnp.dot(before, c_lo[...], preferred_element_type=F32)).astype(BF16)

        @pl.when((g > 0) & (g < groups - 1))
        def _():
            hop_copy().start()

        for d in range(1, subs):
            gather_copy(peer(d)).start()

    def local_work():
        loads[3].wait()
        b_full = bc_in[...]
        b_high = b_full.astype(BF16)
        bc_hi[...] = b_high
        bc_lo[...] = (b_full - b_high.astype(F32)).astype(BF16)
        loads[4].wait()
        loads[5].wait()
        own_block[...] = jnp.dot(bb[...], bk[...], preferred_element_type=F32)
        loads[6].wait()
        loads[7].wait()
        coeffs = sc[...]
        live = lax.broadcasted_iota(jnp.int32, coeffs.shape, 0) < width_ref[0, 0]
        coeffs = jnp.where(live, coeffs, jnp.zeros_like(coeffs))
        fixed[...] = jnp.dot(sb[...], coeffs, preferred_element_type=F32)

    @pl.when(g > 0)
    def _():
        loads[2].wait()
        c_full = c_in[...].T
        high = c_full.astype(BF16)
        c_hi[...] = high
        c_lo[...] = (c_full - high.astype(F32)).astype(BF16)
        local_work()

    owner_only(s, chain)

    @pl.when(g == 0)
    def _():
        loads[2].wait()
        local_work()

    def gather_wait(src):
        remote(v_all.at[src], v_all.at[src], gat_send.at[0], gat_recv.at[src], g, src).wait_recv()

    for d in range(1, subs):
        src = peer(d)
        owner_only(src, lambda src=src: gather_wait(src))
    v = v_all[...].reshape(-1, v_all.shape[2])
    block = own_block[...] + dot_nt(bc_hi[...], v) + dot_nt(bc_lo[...], v)
    cand[2] = block.astype(BF16)
    nb_copies = []
    for i, o in enumerate((0, 1, 3, 4)):
        t = lax.rem(s - o + 2 + subs, subs)
        nb_copies.append(remote(cand.at[2], cand.at[o], nb_send.at[i], nb_recv.at[i], g, t))
    for copy in nb_copies:
        copy.start()
    block_out[0, 0] = cand[2]
    top_out[0] = v.astype(F32).T
    loads[8].wait()
    loads[9].wait()
    for copy in nb_copies:
        copy.wait_recv()
    size = cand.shape[1]
    for a in range(linked.shape[0] // size):
        linked[a * size:(a + 1) * size, :] = cand[adj_ref[0, 0, a]]
    step = result.shape[1]
    for i in range(chunks):
        here = slice(i * step, (i + 1) * step)
        bound = jnp.dot(cm[here, :], linked[...], preferred_element_type=F32)
        interior_out[0, 0, here, :] = (fixed[here, :] + bound).astype(BF16)

    for d in range(1, subs):
        t = peer(d)
        owner_only(t, lambda t=t: piece_copy(t).wait_send())

    if groups > 1:
        @pl.when(g == 0)
        def _():
            for d in range(subs):
                t = peer(d)
                owner_only(t, lambda t=t: ahead_copy(t).wait_send())

    def sent():
        @pl.when((g > 0) & (g < groups - 1))
        def _():
            hop_copy().wait_send()

        for d in range(1, subs):
            gather_copy(peer(d)).wait_send()

    owner_only(s, sent)
    for copy in nb_copies:
        copy.wait_send()


def hand_over_kernel(top, block, interior, top_out, block_out, interior_out, sem):
    copies = []
    half = interior.shape[2] // 2
    pairs = [(top, top_out), (block, block_out)]
    for i in range(2):
        part = (0, 0, pl.ds(i * half, half))
        pairs.append((interior.at[part], interior_out.at[part]))
    for i, (source, target) in enumerate(pairs):
        copies.append(pltpu.make_async_copy(source, target, sem.at[i]))
        copies[-1].start()
    for copy in copies:
        copy.wait()


def hand_over(results):
    hbm = pl.BlockSpec(memory_space=pl.ANY)
    return pl.pallas_call(
        hand_over_kernel,
        out_shape=tuple(jax.ShapeDtypeStruct(r.shape, r.dtype) for r in results),
        in_specs=[hbm] * 3,
        out_specs=(hbm,) * 3,
        scratch_shapes=[pltpu.SemaphoreType.DMA((4,))],
        compiler_params=pltpu.CompilerParams(vmem_limit_bytes=8 * 1024 * 1024),
    )(*results)


def body(*args):
    tb, tc, c, bc, bb, bk, sb, sc, widths, cm, adj = args
    groups, subs = lax.axis_size("grp"), lax.axis_size("sub")
    nt, modes = c.shape[1], tc.shape[2]
    rows = tb.shape[1]
    cols = max(16, modes // subs)
    owners = modes // cols
    lane_rows = max(128, rows)
    per = lane_rows // rows
    nb, ni = bc.shape[2], sb.shape[2]
    slots = adj.shape[2]
    chunks = 4
    hbm = pl.BlockSpec(memory_space=pl.ANY)
    dma = pltpu.SemaphoreType.DMA
    vmem = pltpu.VMEM
    scratch = [
        vmem((lane_rows, tb.shape[2]), BF16),
        vmem(tc.shape[1:], BF16),
        vmem((nt, nt), F32),
        vmem((nt, nt), BF16),
        vmem((nt, nt), BF16),
        vmem((nb, nt), F32),
        vmem((nb, nt), BF16),
        vmem((nb, nt), BF16),
        vmem(bb.shape[2:], BF16),
        vmem(bk.shape[2:], BF16),
        vmem((nb, modes), F32),
        vmem(sb.shape[2:], BF16),
        vmem(sc.shape[2:], BF16),
        vmem(cm.shape[2:], BF16),
        vmem((ni, modes), F32),
        vmem((owners, cols, lane_rows), F32),
        vmem((subs, cols, lane_rows), F32),
        vmem((cols, nt), BF16),
        vmem((owners, cols, nt), BF16),
        vmem((nt, modes), F32),
        vmem((5, nb, modes), BF16),
        vmem((slots * nb, modes), BF16),
        vmem((chunks, ni // chunks, modes), BF16),
        dma((10,)),
        dma((chunks + 2,)),
        dma((owners,)),
        dma((subs,)),
        dma,
        dma,
        dma((subs,)),
        dma((owners,)),
        dma((4,)),
        dma((4,)),
        vmem((subs, cols, lane_rows), F32),
        dma((owners,)),
        dma((subs,)),
        pltpu.SMEM(adj.shape, jnp.int32),
    ]
    results = pl.pallas_call(
        functools.partial(kernel, groups, subs, owners),
        out_shape=(
            jax.ShapeDtypeStruct((1, nt, modes), F32),
            jax.ShapeDtypeStruct((1, 1, nb, modes), BF16),
            jax.ShapeDtypeStruct((1, 1, ni, modes), BF16),
        ),
        in_specs=[hbm, hbm, hbm, hbm, hbm, hbm, hbm, hbm, pl.BlockSpec(memory_space=pltpu.SMEM), hbm, hbm],
        out_specs=(pl.BlockSpec(memory_space=pltpu.VMEM),) * 3,
        scratch_shapes=scratch,
        compiler_params=pltpu.CompilerParams(
            collective_id=0, has_side_effects=True, vmem_limit_bytes=24 * 1024 * 1024
        ),
        cost_estimate=pl.CostEstimate(flops=500_000_000, bytes_accessed=5_000_000, transcendentals=0),
    )(*[pltpu.with_memory_space_constraint(a, pltpu.HBM) if a.ndim > 2 else a for a in args])
    return hand_over(results)


def solution(mesh):
    placed = (
        P("grp", "sub", None),
        P("grp", None, None),
        P("grp", None, None),
        P("grp", "sub", None, None),
        P("grp", "sub", None, None),
        P("grp", "sub", None, None),
        P("grp", "sub", None, None),
        P("grp", "sub", None, None),
        P("grp", "sub"),
        P("grp", "sub", None, None),
        P("grp", "sub", None),
    )
    return jax.shard_map(
        body,
        mesh=mesh,
        in_specs=placed,
        out_specs=(P("grp", None, None), P("grp", "sub", None, None), P("grp", "sub", None, None)),
        check_vma=False,
    )
```
